512 devices in a mesh: outer: 64 (over x, y_hi, z), node: 8 (over y_lo, core).
Axes of the slice: x: 4, y: 8 (y_hi: 2, y_lo: 4; y = y_hi * 4 + y_lo), z: 8, core: 2. Of those that a mesh axis runs over, the one named last changes fastest.
Arguments:
- hidden: bfloat16 [131072, 4096], P(('outer', 'node')), may hold values from -24 to 24
- codes: bfloat16 [4096, 256], P(('node', 'outer')), may hold values from -4 to 4
- scales: float32 [2, 256], replicated, may hold values from 0.008 to 0.032
- cotangent: bfloat16 [131072, 256], P(('outer', 'node')), may hold values from -6 to 6
Outputs:
- projected: bfloat16 [131072, 256], P(('outer', 'node'))
- grad_hidden: bfloat16 [131072, 4096], P(('outer', 'node'))
- grad_weight: float32 [4096, 256], P(('node', 'outer'))
The draws below stay inside these ranges and needn't reach their ends.
All inputs are finite; a program needn't handle non-finite values.
Results may differ from the reference program's by a relative error of at most 0.017.
Values may be sent and summed in bfloat16 or wider, within the bound.
No kernel may reach another device: no remote copies, remote signals or barrier semaphores. Data moves between devices by JAX's collectives and lax.ppermute only.
A program may use at most 64 MiB of HBM per device.

```python
import math
import jax
import jax.numpy as jnp
from jax import lax

D = 4096
BLOCK = 2048
TOK_DEV = 256
COLS = 256
NBLOCKS = 2
TOKENS = 131072
N_OUTER = 64
N_NODE = 8


def with_spikes(values, key, source, target, shards_of, factor):
    def block_of(axis_at):
        return (jnp.arange(values.shape[axis_at]) // (values.shape[axis_at] // shards_of)).reshape((-1,) + (1,) * (values.ndim - 1 - axis_at))

    first = jax.random.permutation(key, shards_of)[block_of(target)]
    second = (block_of(target) + shards_of // 2) % shards_of
    return jnp.where((block_of(source) == first) | (block_of(source) == second), factor * values, values)


def level_of(stream_key, shape, cuts, low, high):
    factor_of = 1.0
    for axis_at, shards_of in cuts:
        steps = jax.random.uniform(jax.random.fold_in(jax.random.fold_in(stream_key, 6), axis_at), (shards_of,), jnp.float32, low / len(cuts), high / len(cuts))
        factor_of = factor_of * jnp.repeat(jnp.exp(steps), shape[axis_at] // shards_of).reshape((-1,) + (1,) * (len(shape) - 1 - axis_at))
    return factor_of


def gaussian(own_key, dims, scale, reach, split=(), kind=jnp.bfloat16):
    drawn = scale * jax.random.normal(own_key, dims, jnp.float32)
    if split:
        drawn = drawn * level_of(own_key, dims, split, -0.22, 0.18)
    return jnp.clip(drawn, -reach, reach).astype(kind)


def noise_with(key, dims, scale, reach, cuts, heavy, kind=jnp.bfloat16):
    values = scale * jax.random.normal(key, dims, jnp.float32)
    if cuts:
        values = values * level_of(key, dims, cuts, -0.22, 0.18)
    return jnp.clip(with_spikes(values, jax.random.fold_in(key, 3), *heavy), -reach, reach).astype(kind)


def setup_inputs(seed: int = 0) -> dict:
    key_list = jax.random.split(jax.random.key(seed), 5)
    hidden = noise_with(key_list[0], (TOKENS, D), 1.0, 24.0, ((0, 512),), (0, 1, 512, 6.0))
    codes = gaussian(key_list[1], (D, COLS), 1.0, 4.0, ((0, 512),))
    scales = jnp.clip(jnp.exp(jax.random.uniform(key_list[2], (NBLOCKS, COLS), jnp.float32, math.log(0.008), math.log(0.032))), 0.008, 0.032)
    cotangent = gaussian(key_list[3], (TOKENS, COLS), 1.0, 6.0, ((0, 512),))
    return {"hidden": hidden, "codes": codes, "scales": scales, "cotangent": cotangent}


def dequantize(codes, scales):
    row_scales = jnp.repeat(scales, BLOCK, axis=0)
    return (codes.astype(jnp.float32) * row_scales).astype(jnp.bfloat16)


def reference(hidden, codes, scales, cotangent):
    weight = dequantize(codes, scales)
    projected = jnp.dot(hidden, weight, preferred_element_type=jnp.float32).astype(jnp.bfloat16)
    grad_hidden = lax.dot_general(cotangent, weight, (((1,), (1,)), ((), ())), preferred_element_type=jnp.float32).astype(jnp.bfloat16)
    hid_blocks = hidden.reshape(N_OUTER, N_NODE, TOK_DEV, D)
    cot_blocks = cotangent.reshape(N_OUTER, N_NODE, TOK_DEV, COLS)

    def add_term(total, pair):
        term = lax.dot_general(pair[0], pair[1], (((0,), (0,)), ((), ())), preferred_element_type=jnp.float32)
        term = lax.optimization_barrier(term.astype(jnp.bfloat16))
        return total + term.astype(jnp.float32), None

    def add_group(total, pair):
        group, unused = lax.scan(add_term, jnp.zeros((D, COLS), jnp.float32), pair)
        group = lax.optimization_barrier(group.astype(jnp.bfloat16))
        return total + group.astype(jnp.float32), None

    grad_weight, unused = lax.scan(add_group, jnp.zeros((D, COLS), jnp.float32), (hid_blocks, cot_blocks))
    return projected, grad_hidden, grad_weight
```

```python
import jax
import jax.numpy as jnp
from jax import lax
from jax.sharding import Mesh, PartitionSpec as P

BLOCK = 2048
TORUS = ("yl", "yh", "z")


def exchange(pieces, axis):
    return lax.all_to_all(pieces, axis, 0, 0, tiled=True)


def swap(value):
    return lax.ppermute(value, "c", [(0, 1), (1, 0)])


def body(hidden, codes, scales, cotangent):
    tokens, width = hidden.shape
    rows, cols = codes.shape
    core = lax.axis_index("c")
    f32, bf16 = jnp.float32, jnp.bfloat16

    start = (lax.axis_index("yl") * 2 + core) * (width // 8)
    scale = lax.dynamic_index_in_dim(scales, start // BLOCK, 0, keepdims=True)
    own = (codes.astype(f32) * scale).astype(bf16)
    plane = exchange(jnp.broadcast_to(own[None], (64, rows, cols)), TORUS)
    plane = plane.reshape(1, 64 * rows, cols)
    half = exchange(jnp.broadcast_to(plane, (4,) + plane.shape[1:]), "x")
    half = half.reshape(4, 4, 16 * rows, cols).transpose(1, 0, 2, 3).reshape(4, width // 8, cols)
    other = swap(half)

    parts = hidden.reshape(tokens, 4, 2, width // 8)
    keep = lax.dynamic_index_in_dim(parts, core, 2, keepdims=False).reshape(tokens, width // 2)
    give = lax.dynamic_index_in_dim(parts, 1 - core, 2, keepdims=False).reshape(tokens, width // 2)
    got = swap(give)
    cot_other = swap(cotangent)
    both = jnp.concatenate([keep, got], axis=0)
    cots = jnp.concatenate([cotangent, cot_other], axis=0)
    term = lax.dot_general(both, cots, (((0,), (0,)), ((), ())), preferred_element_type=f32).astype(bf16)
    term = term.reshape(4, 4, 16 * rows, cols).transpose(1, 0, 2, 3).reshape(4, 64 * rows, cols)
    sums = jnp.sum(exchange(term, "x").astype(f32), axis=0).astype(bf16)
    grad_weight = jnp.sum(exchange(sums.reshape(64, rows, cols), TORUS).astype(f32), axis=0)

    first = jnp.where(core == 0, half, other)
    second = jnp.where(core == 0, other, half)
    whole = jnp.stack([first, second], axis=1).reshape(width, cols)
    projected = jnp.dot(hidden, whole, preferred_element_type=f32).astype(bf16)
    grad_hidden = lax.dot_general(
        cotangent, whole, (((1,), (1,)), ((), ())), preferred_element_type=f32
    ).astype(bf16)
    return projected, grad_hidden, grad_weight


def solution(mesh):
    fine = Mesh(mesh.devices.reshape(4, 2, 8, 4, 2), ("x", "yh", "z", "yl", "c"))
    outer, node = ("x", "yh", "z"), ("yl", "c")
    tokens, rows = P(outer + node, None), P(node + outer, None)
    return jax.shard_map(
        body,
        mesh=fine,
        in_specs=(tokens, rows, P(), tokens),
        out_specs=(tokens, tokens, rows),
        check_vma=False,
    )
```

```python
import functools

import jax
import jax.numpy as jnp
from jax import lax
from jax.experimental import pallas as pl
from jax.experimental.pallas import tpu as pltpu
from jax.sharding import Mesh, PartitionSpec as P

BLOCK = 2048
TORUS = ("yl", "yh", "z")
VMEM_BYTES = 32 * 1024 * 1024
F32, BF16 = jnp.float32, jnp.bfloat16
ANY = pl.BlockSpec(memory_space=pl.ANY)
VMEM = pl.BlockSpec(memory_space=pltpu.VMEM)


def exchange(pieces, axis):
    return lax.all_to_all(pieces, axis, 0, 0, tiled=True)


def swap(value):
    return lax.ppermute(value, "c", [(0, 1), (1, 0)])


def call(kernel, out_shape, in_specs, out_specs, scratch, flops, moved, aliases=None):
    return pl.pallas_call(
        kernel,
        out_shape=out_shape,
        in_specs=in_specs,
        out_specs=out_specs,
        scratch_shapes=scratch,
        input_output_aliases=aliases or {},
        compiler_params=pltpu.CompilerParams(vmem_limit_bytes=VMEM_BYTES),
        cost_estimate=pl.CostEstimate(flops=flops, bytes_accessed=moved, transcendentals=0),
    )


def columns(part, core, share):
    return pl.ds(pl.multiple_of((part * 2 + core) * share, share), share)


def prepare(hidden, codes, scales, cotangent, copies, give, sems):
    tokens, width = hidden.shape
    share = width // 8
    other = 1 - lax.axis_index("c")
    sends = []
    for part in range(4):
        sends.append(
            pltpu.make_async_copy(
                hidden.at[:, columns(part, other, share)],
                give.at[:, pl.ds(part * share, share)],
                sems.at[part],
            )
        )
    sends.append(pltpu.make_async_copy(cotangent, give.at[:, pl.ds(4 * share, cotangent.shape[1])], sems.at[4]))
    for send in sends:
        send.start()
    scale = jnp.where(lax.axis_index("yl") * (2 * share) >= BLOCK, scales[1:2, :], scales[0:1, :])
    own = (codes[...].astype(F32) * scale).astype(BF16)
    twice = jnp.concatenate([own, own], axis=0)
    for at in range(0, copies.shape[0], 16):
        copies[at : at + 16, :] = twice
    for send in sends:
        send.wait()


def pair_terms(hidden, cotangent, got, term, own_cols, got_cols, own_cot, got_cot, out, load_sems, cot_sems, out_sems):
    tokens, width = hidden.shape
    share = width // 8
    core = lax.axis_index("c")
    cots = [
        pltpu.make_async_copy(cotangent, own_cot, cot_sems.at[0]),
        pltpu.make_async_copy(got.at[:, pl.ds(4 * share, cotangent.shape[1])], got_cot, cot_sems.at[1]),
    ]
    loads = []
    for part in range(4):
        loads.append(
            (
                pltpu.make_async_copy(
                    hidden.at[:, columns(part, core, share)], own_cols.at[part], load_sems.at[part, 0]
                ),
                pltpu.make_async_copy(
                    got.at[:, pl.ds(part * share, share)], got_cols.at[part], load_sems.at[part, 1]
                ),
            )
        )
    for copy in cots:
        copy.start()
    for pair in loads:
        for copy in pair:
            copy.start()
    for copy in cots:
        copy.wait()
    stores = []
    dims = (((0,), (0,)), ((), ()))
    for part in range(4):
        for copy in loads[part]:
            copy.wait()
        total = lax.dot_general(own_cols[part], own_cot[...], dims, preferred_element_type=F32)
        total += lax.dot_general(got_cols[part], got_cot[...], dims, preferred_element_type=F32)
        out[:, part] = total.astype(BF16).reshape(out.shape[0], out.shape[2], out.shape[3])
        store = pltpu.make_async_copy(out.at[:, part], term.at[:, part], out_sems.at[part])
        store.start()
        stores.append(store)
    for store in stores:
        store.wait()


def weight_half(which, hidden, cotangent, weight, *rest):
    if which == 0:
        acc_out, grad, cols, pieces, cot, out, load_sems, cot_sem, out_sems = rest
    else:
        acc_in, grad_in, acc_out, grad, cols, pieces, cot, out, load_sems, cot_sem, out_sems = rest
    tokens, width = hidden.shape
    share = width // 8
    core = lax.axis_index("c")
    if which == 1:
        core = 1 - core
    cot_load = pltpu.make_async_copy(cotangent, cot, cot_sem.at[0])
    loads = []
    for part in range(4):
        loads.append(
            (
                pltpu.make_async_copy(weight.at[:, part], pieces.at[part], load_sems.at[part, 0]),
                pltpu.make_async_copy(hidden.at[:, columns(part, core, share)], cols.at[part], load_sems.at[part, 1]),
            )
        )
    cot_load.start()
    for pair in loads:
        for copy in pair:
            copy.start()
    cot_load.wait()
    stores = []
    if which == 0:
        total = jnp.zeros(acc_out.shape, F32)
    else:
        total = acc_in[...]
    for part in range(4):
        for copy in loads[part]:
            copy.wait()
        rows = pieces[part].reshape(share, weight.shape[3])
        out[part] = lax.dot_general(
            cot[...], rows, (((1,), (1,)), ((), ())), preferred_element_type=F32
        ).astype(BF16)
        store = pltpu.make_async_copy(out.at[part], grad.at[:, columns(part, core, share)], out_sems.at[part])
        store.start()
        stores.append(store)
        total += jnp.dot(cols[part], rows, preferred_element_type=F32)
    acc_out[...] = total.astype(acc_out.dtype)
    for store in stores:
        store.wait()


def body(hidden, codes, scales, cotangent):
    tokens, width = hidden.shape
    rows, cols = codes.shape
    share = width // 8
    piece = share // 4
    dma = pltpu.SemaphoreType.DMA
    sds = jax.ShapeDtypeStruct
    half_flops = 2 * tokens * (width // 2) * cols

    copies, give = call(
        prepare,
        (sds((64 * rows, cols), BF16), sds((tokens, width // 2 + cols), BF16)),
        [ANY, VMEM, VMEM, ANY],
        (VMEM, ANY),
        [dma((5,))],
        0,
        3 << 20,
    )(hidden, codes, scales, cotangent)
    got = swap(give)
    plane = exchange(copies.reshape(64, rows, cols), TORUS)

    term = call(
        pair_terms,
        sds((4, 4, piece, cols), BF16),
        [ANY, ANY, ANY],
        ANY,
        [
            pltpu.VMEM((4, tokens, share), BF16),
            pltpu.VMEM((4, tokens, share), BF16),
            pltpu.VMEM((tokens, cols), BF16),
            pltpu.VMEM((tokens, cols), BF16),
            pltpu.VMEM((4, 4, piece, cols), BF16),
            dma((4, 2)),
            dma((2,)),
            dma((4,)),
        ],
        2 * half_flops,
        4 << 20,
    )(hidden, cotangent, got)
    sums = exchange(term.reshape(4, 4 * piece, cols), "x")

    plane, term = lax.optimization_barrier((plane, term))
    half = exchange(jnp.broadcast_to(plane.reshape(1, 4 * piece, cols), (4, 4 * piece, cols)), "x")
    half = half.reshape(4, 4, piece, cols)
    other = swap(half)

    sums = jnp.sum(sums.astype(F32), axis=0).astype(BF16)
    grad_weight = jnp.sum(exchange(sums.reshape(64, rows, cols), TORUS).astype(F32), axis=0)

    scratch = [
        pltpu.VMEM((4, tokens, share), BF16),
        pltpu.VMEM((4, 4, piece, cols), BF16),
        pltpu.VMEM((tokens, cols), BF16),
        pltpu.VMEM((4, tokens, share), BF16),
        dma((4, 2)),
        dma((1,)),
        dma((4,)),
    ]
    part, grad = call(
        functools.partial(weight_half, 0),
        (sds((tokens, cols), F32), sds((tokens, width), BF16)),
        [ANY, ANY, ANY],
        (VMEM, ANY),
        scratch,
        2 * half_flops,
        4 << 20,
    )(hidden, cotangent, half)
    projected, grad_hidden = call(
        functools.partial(weight_half, 1),
        (sds((tokens, cols), BF16), sds((tokens, width), BF16)),
        [ANY, ANY, ANY, VMEM, ANY],
        (VMEM, ANY),
        scratch,
        2 * half_flops,
        4 << 20,
        {4: 1},
    )(hidden, cotangent, other, part, grad)
    return projected, grad_hidden, grad_weight


def solution(mesh):
    fine = Mesh(mesh.devices.reshape(4, 2, 8, 4, 2), ("x", "yh", "z", "yl", "c"))
    outer, node = ("x", "yh", "z"), ("yl", "c")
    tokens, rows = P(outer + node, None), P(node + outer, None)
    return jax.shard_map(
        body,
        mesh=fine,
        in_specs=(tokens, rows, P(), tokens),
        out_specs=(tokens, tokens, rows),
        check_vma=False,
    )
```

```python
import functools

import jax
import jax.numpy as jnp
from jax import lax
from jax.experimental import pallas as pl
from jax.experimental.pallas import tpu as pltpu
from jax.sharding import Mesh, PartitionSpec as P

BLOCK = 2048
TORUS = ("yh", "z", "yl")
VMEM_BYTES = 32 * 1024 * 1024
F32, BF16 = jnp.float32, jnp.bfloat16
HBM = pl.BlockSpec(memory_space=pltpu.HBM)
ANY = pl.BlockSpec(memory_space=pl.ANY)
VMEM = pl.BlockSpec(memory_space=pltpu.VMEM)


def exchange(pieces):
    return lax.all_to_all(pieces, TORUS, 0, 0, tiled=True)


def swap(value):
    return lax.ppermute(value, "c", [(0, 1), (1, 0)])


def along_x(value, shift):
    return lax.ppermute(value, "x", [(at, (at + shift) % 4) for at in range(4)])


def call(kernel, out_shape, in_specs, out_specs, scratch, flops, moved, aliases=None, limit=VMEM_BYTES):
    return pl.pallas_call(
        kernel,
        out_shape=out_shape,
        in_specs=in_specs,
        out_specs=out_specs,
        scratch_shapes=scratch,
        input_output_aliases=aliases or {},
        compiler_params=pltpu.CompilerParams(vmem_limit_bytes=limit),
        cost_estimate=pl.CostEstimate(flops=flops, bytes_accessed=moved, transcendentals=0),
    )


def columns(part, core, share):
    return pl.ds(pl.multiple_of((part * 2 + core) * share, share), share)


def prepare(hidden, codes, scales, cotangent, copies, give, code_buf, scale_buf, copy_buf, give_buf, load_sems, store_sems):
    width = hidden.shape[1]
    share = width // 8
    other = 1 - lax.axis_index("c")
    edge = pl.ds(4 * share, cotangent.shape[1])
    loads, stores = [], []
    for part in range(4):
        slot = pl.ds(part * share, share)
        loads.append(
            pltpu.make_async_copy(hidden.at[:, columns(part, other, share)], give_buf.at[:, slot], load_sems.at[part])
        )
        stores.append(pltpu.make_async_copy(give_buf.at[:, slot], give.at[:, slot], store_sems.at[part]))
    loads.append(pltpu.make_async_copy(cotangent, give_buf.at[:, edge], load_sems.at[4]))
    stores.append(pltpu.make_async_copy(give_buf.at[:, edge], give.at[:, edge], store_sems.at[4]))
    small = [
        pltpu.make_async_copy(codes, code_buf, load_sems.at[5]),
        pltpu.make_async_copy(scales, scale_buf, load_sems.at[6]),
    ]
    for copy in small + loads:
        copy.start()
    for copy in small:
        copy.wait()
    scale = jnp.where(lax.axis_index("yl") * (2 * share) >= BLOCK, scale_buf[1:2, :], scale_buf[0:1, :])
    own = (code_buf[...].astype(F32) * scale).astype(BF16)
    twice = jnp.concatenate([own, own], axis=0)
    for at in range(0, copies.shape[0], 16):
        copy_buf[at : at + 16, :] = twice
    stores.append(pltpu.make_async_copy(copy_buf, copies, store_sems.at[5]))
    stores[5].start()
    for load, store in zip(loads, stores):
        load.wait()
        store.start()
    for store in stores:
        store.wait()


def pair_terms(hidden, cotangent, got, term0, term1, term2, term3, outs, sems):
    share = hidden.shape[1] // 8
    piece = share // 4
    core, me = lax.axis_index("c"), lax.axis_index("x")
    dims = (((0,), (0,)), ((), ()))
    got_cot = got[:, 4 * share :]
    stores = []
    for shift, term in ((2, term2), (1, term1), (3, term3), (0, term0)):
        at = lax.rem(me + shift, 4) * piece
        for part in range(4):
            mine = pl.ds(pl.multiple_of((part * 2 + core) * share + at, piece), piece)
            theirs = pl.ds(pl.multiple_of(part * share + at, piece), piece)
            total = lax.dot_general(hidden[:, mine], cotangent[...], dims, preferred_element_type=F32)
            total += lax.dot_general(got[:, theirs], got_cot, dims, preferred_element_type=F32)
            outs[shift, :, part] = total.astype(BF16).reshape(outs.shape[1], outs.shape[3], outs.shape[4])
        store = pltpu.make_async_copy(outs.at[shift], term, sems.at[shift])
        store.start()
        stores.append(store)
    for store in stores:
        store.wait()


def assemble(piece0, piece1, piece2, piece3, rows):
    me = lax.axis_index("x")
    blocks, _, height, _ = piece0.shape
    for shift, source in enumerate((piece0, piece1, piece2, piece3)):
        at = lax.rem(me + 4 - shift, 4) * (blocks * height)
        for part in range(4):
            for block in range(0, blocks, 2):
                start = pl.multiple_of(at + block * height, 2 * height)
                rows[part, pl.ds(start, 2 * height), :] = jnp.concatenate(
                    [source[block, part], source[block + 1, part]], axis=0
                )


def weight_half(which, hidden, cotangent, rows, *rest):
    if which == 0:
        acc_out, grad, out, out_sems = rest
        total = jnp.zeros(acc_out.shape, F32)
    else:
        acc_in, grad_in, acc_out, grad, out, out_sems = rest
        total = acc_in[...]
    share = hidden.shape[1] // 8
    core = lax.axis_index("c")
    if which == 1:
        core = 1 - core
    stores = []
    for part in range(4):
        out[part] = lax.dot_general(
            cotangent[...], rows[part], (((1,), (1,)), ((), ())), preferred_element_type=F32
        ).astype(BF16)
        store = pltpu.make_async_copy(out.at[part], grad.at[:, columns(part, core, share)], out_sems.at[part])
        store.start()
        stores.append(store)
        total += jnp.dot(hidden[:, columns(part, core, share)], rows[part], preferred_element_type=F32)
    acc_out[...] = total.astype(acc_out.dtype)
    for store in stores:
        store.wait()


def body(hidden, codes, scales, cotangent):
    tokens, width = hidden.shape
    rows, cols = codes.shape
    share = width // 8
    piece = share // 4
    dma = pltpu.SemaphoreType.DMA
    sds = jax.ShapeDtypeStruct
    half_flops = 2 * tokens * (width // 2) * cols

    copies, give = call(
        prepare,
        (sds((64 * rows, cols), BF16), sds((tokens, width // 2 + cols), BF16)),
        [HBM, HBM, HBM, HBM],
        (HBM, HBM),
        [
            pltpu.VMEM((rows, cols), BF16),
            pltpu.VMEM((2, cols), F32),
            pltpu.VMEM((64 * rows, cols), BF16),
            pltpu.VMEM((tokens, width // 2 + cols), BF16),
            dma((7,)),
            dma((6,)),
        ],
        0,
        3 << 20,
        limit=61 * 1024 * 1024,
    )(hidden, codes, scales, cotangent)
    got = swap(give)
    plane = exchange(copies.reshape(64, rows, cols))

    terms = call(
        pair_terms,
        [sds((16, 4, rows, cols), BF16)] * 4,
        [VMEM, VMEM, VMEM],
        [HBM] * 4,
        [pltpu.VMEM((4, 16, 4, rows, cols), BF16), dma((4,))],
        2 * half_flops,
        4 << 20,
    )(hidden, cotangent, got)
    t2, t1, t3 = [along_x(terms[shift], shift) for shift in (2, 1, 3)]
    plane, terms = lax.optimization_barrier((plane, terms))
    plane = plane.reshape(16, 4, rows, cols)
    p3, p2, p1 = [along_x(plane, shift) for shift in (3, 2, 1)]
    sums = terms[0].astype(F32)
    for value in (t1, t2, t3):
        sums += value.astype(F32)
    sums = sums.astype(BF16).reshape(64, rows, cols)
    blocks = exchange(sums)
    mine = call(
        assemble,
        sds((4, share, cols), BF16),
        [VMEM] * 4,
        VMEM,
        [],
        0,
        2 << 20,
    )(plane, p1, p2, p3)
    other = swap(mine)

    scratch = [
        pltpu.VMEM((4, tokens, share), BF16),
        dma((4,)),
    ]
    part, grad = call(
        functools.partial(weight_half, 0),
        (sds((tokens, cols), F32), sds((tokens, width), BF16)),
        [VMEM] * 3,
        (VMEM, HBM),
        scratch,
        200 * half_flops,
        4 << 20,
    )(hidden, cotangent, mine)
    projected, grad_hidden = call(
        functools.partial(weight_half, 1),
        (sds((tokens, cols), BF16), sds((tokens, width), BF16)),
        [VMEM] * 4 + [HBM],
        (VMEM, HBM),
        scratch,
        2 * half_flops,
        4 << 20,
        {4: 1},
    )(hidden, cotangent, other, part, grad)
    blocks, projected = lax.optimization_barrier((blocks, projected))
    grad_weight = jnp.sum(blocks.astype(F32), axis=0)
    return projected, grad_hidden, grad_weight


def solution(mesh):
    fine = Mesh(mesh.devices.reshape(4, 2, 8, 4, 2), ("x", "yh", "z", "yl", "c"))
    outer, node = ("x", "yh", "z"), ("yl", "c")
    tokens, rows = P(outer + node, None), P(node + outer, None)
    return jax.shard_map(
        body,
        mesh=fine,
        in_specs=(tokens, rows, P(), tokens),
        out_specs=(tokens, tokens, rows),
        check_vma=False,
    )
```
